32 devices in a mesh: member: 2 (over x), wave: 8 (over z, y), lev: 2 (over core).
Axes of the slice: x: 2, y: 2, z: 4, core: 2. Of those that a mesh axis runs over, the one named last changes fastest.
Arguments:
- grid: bfloat16 [128, 320, 2, 1280], P(('member', 'lev'), 'wave'), parts along dimension 0, may hold values from -6 to 6
- lat_order: int32 [320], replicated, may hold values from 0 to 319, each once
- wave_order: int32 [640], replicated, may hold values from 0 to 639, as said below
- trim: int32 [640], replicated, may hold values from 0 to 4, as said below
- legendre: bfloat16 [640, 640, 320], P('wave'), may hold values from -0.3125 to 0.3125
- modes_in: bfloat16 [64, 64], replicated, may hold values from -0.75 to 0.75
- modes_out: bfloat16 [64, 64], replicated, may hold values from -0.75 to 0.75
- implicit: float32 [64], replicated, may hold values from 0.3 to 30
Outputs:
- fourier_out: bfloat16 [128, 320, 2, 1280], P(('member', 'lev'), 'wave'), parts along dimension 0
The draws below stay inside these ranges and needn't reach their ends.
There are 2 independent parts, one for each index of `member`. The reference program is written for one: setup_inputs(seed, part) draws one part's arguments, and reference() takes and returns one part's arrays. A program takes and returns all parts, laid end to end along the dimension named above; an argument that names none is the same for every part. Nothing has to cross between parts.
Inputs may be any that keep to these rules, and one draw needn't show every extreme that they name: `wave_order`: a permutation of 0 to 639 in which entries 2i and 2i+1 are k and 639-k for some k. `trim`: for wavenumber m, how many blocks of 64 latitudes nearest each pole take no part in its products.
All inputs are finite; a program needn't handle non-finite values.
Results may differ from the reference program's by a relative error of at most 0.015.
Values may be sent and summed in bfloat16 or wider, within the bound.
A program may use at most 192 MiB of HBM per device.

```python
import math
import jax
import jax.numpy as jnp
from jax import lax

F = 64
NLON = 1280
M = 640
HALF = 320
LBLK = 64


def draw_wave_order(key, part):
    pair_first = jax.random.permutation(key, M // 2).astype(jnp.int32)
    return jnp.stack([pair_first, M - 1 - pair_first], 1).reshape(M).astype(jnp.int32)


def draw_trim(key, part):
    blocks = HALF // LBLK
    base_blocks = jnp.arange(M, dtype=jnp.int32) * blocks // M
    jitter = jax.random.randint(jax.random.fold_in(key, 7), (M,), 0, 2, dtype=jnp.int32)
    drawn_trim = jnp.clip(base_blocks - jitter, 0, blocks - 1)
    return drawn_trim.at[M - 1].set(blocks - 1).astype(jnp.int32)


def block_scale(rng, extent, cuts, low, largest):
    gain, own = 1.0, jax.random.fold_in(rng, 6)
    for position, parts in cuts:
        draws = jnp.exp(jax.random.uniform(jax.random.fold_in(own, position), (parts,), jnp.float32, low / len(cuts), largest / len(cuts)))
        gain = gain * jnp.repeat(draws, extent[position] // parts).reshape([-1 if axis == position else 1 for axis in range(len(extent))])
    return gain


def gaussian(stream_key, shape, scale, bound, shards=(), kind=jnp.bfloat16):
    drawn = jax.random.normal(stream_key, shape, jnp.float32) * scale
    if len(shards) > 0:
        drawn = block_scale(stream_key, shape, shards, -0.22, 0.18) * drawn
    return jnp.clip(drawn, min=-bound, max=bound).astype(kind)


def setup_inputs(seed: int = 0, part: int = 0) -> dict:
    keys = jax.random.split(jax.random.key(seed), 9)
    part_splits = jax.random.split(jax.random.fold_in(keys[8], part), 9)
    return {
        "grid": gaussian(part_splits[0], (F, HALF, 2, NLON), 1.0, 6.0, ((0, 2), (1, 8))),
        "lat_order": jax.random.permutation(keys[1], HALF).astype(jnp.int32),
        "wave_order": draw_wave_order(jax.random.fold_in(keys[8], 71), part),
        "trim": draw_trim(jax.random.fold_in(keys[8], 71), part),
        "legendre": gaussian(keys[4], (M, M, HALF), HALF ** -0.5, 0.3125, ((0, 8),)),
        "modes_in": gaussian(keys[5], (F, F), F ** -0.5, 0.75),
        "modes_out": gaussian(keys[6], (F, F), F ** -0.5, 0.75),
        "implicit": jnp.clip(jnp.exp(jax.random.uniform(keys[7], (F,), jnp.float32, math.log(0.3), math.log(30.0))), 0.3, 30.0),
    }


def reference(grid, lat_order, wave_order, trim, legendre, modes_in, modes_out, implicit):
    spectra = jnp.fft.rfft(grid.astype(jnp.float32), axis=3)[..., :M] / math.sqrt(NLON)
    picked = spectra[..., wave_order]
    fourier = jnp.stack([jnp.real(picked), jnp.imag(picked)], -1).reshape(F, HALF, 2, 2 * M).astype(jnp.bfloat16)
    fourier = lax.optimization_barrier(fourier).astype(jnp.float32)
    symmetric = jnp.stack([fourier[:, :, 0] + fourier[:, :, 1], fourier[:, :, 0] - fourier[:, :, 1]], 2).astype(jnp.bfloat16)
    inverse_order = jnp.zeros((HALF,), jnp.int32).at[lat_order].set(jnp.arange(HALF, dtype=jnp.int32))
    physical = symmetric[:, inverse_order]
    latitude = jnp.arange(HALF, dtype=jnp.int32)
    row_index = jnp.arange(M, dtype=jnp.int32)

    def one_slot(slot_index):
        wavenum = wave_order[slot_index]
        keep_mask = (wavenum + row_index < M)[:, None] & (latitude >= LBLK * trim[wavenum])[None, :]
        lat_basis = jnp.where(keep_mask, legendre[slot_index].astype(jnp.float32), jnp.float32(0.0)).reshape(M // 2, 2, HALF)
        slot_data = lax.dynamic_slice_in_dim(physical, 2 * slot_index, 2, 3).astype(jnp.float32)
        coeffs = jnp.einsum('aej,fjec->aecf', lat_basis, slot_data).astype(jnp.bfloat16)
        degree = (wavenum + row_index).astype(jnp.float32).reshape(M // 2, 2)
        factor = degree * (degree + 1.0) / float(M * (M - 1))
        modal_part = jnp.einsum('kl,aecl->aeck', modes_in.astype(jnp.float32), coeffs.astype(jnp.float32))
        scaled = (modal_part / (1.0 + factor[:, :, None, None] * implicit)).astype(jnp.bfloat16)
        solved = jnp.einsum('lk,aeck->aecl', modes_out.astype(jnp.float32), scaled.astype(jnp.float32)).astype(jnp.bfloat16)
        parity_sums = jnp.einsum('aej,aecl->ejcl', lat_basis, solved.astype(jnp.float32))
        hemispheres = jnp.stack([parity_sums[0] + parity_sums[1], parity_sums[0] - parity_sums[1]], 1)
        return hemispheres.astype(jnp.bfloat16)
    results = lax.map(one_slot, jnp.arange(M, dtype=jnp.int32))
    ordered = results[:, lat_order]
    return ordered.transpose(4, 1, 2, 0, 3).reshape(F, HALF, 2, 2 * M)
```

```python
import functools
import math

import jax
import jax.numpy as jnp
from jax import lax
from jax.experimental import pallas as pl
from jax.experimental.pallas import tpu as pltpu
from jax.sharding import PartitionSpec as P

LBLK = 64
LANES = 128
F32 = jnp.float32
BF16 = jnp.bfloat16


def dft_kernel(slots, block, grid_ref, cos_a, sin_a, cos_b, sin_b, out_ref, table, held):
    step = pl.program_id(0)
    waves = cos_b.shape[0]
    fields = grid_ref.shape[0]
    width = 2 * fields

    @pl.when(step == 0)
    def _():
        for a in range(cos_a.shape[1]):
            ca, sa = cos_a[:, a : a + 1], sin_a[:, a : a + 1]
            cols = slice(a * LANES, (a + 1) * LANES)
            table[:waves, cols] = (ca * cos_b[...] - sa * sin_b[...]).astype(BF16)
            table[waves:, cols] = (-(sa * cos_b[...] + ca * sin_b[...])).astype(BF16)

    rows = jnp.concatenate(
        [grid_ref[:, s].reshape(width, grid_ref.shape[3]) for s in range(block)], 0
    )
    real = lax.dot_general(
        table[:waves], rows, (((1,), (1,)), ((), ())), preferred_element_type=F32
    )
    imag = lax.dot_general(
        table[waves:], rows, (((1,), (1,)), ((), ())), preferred_element_type=F32
    )
    for s in range(block):
        part = slice(s * width, (s + 1) * width)
        both = jnp.concatenate([real[:, part], imag[:, part]], 1)
        held[pl.ds(step * block + s, waves, stride=slots), :] = both

    @pl.when(step == pl.num_programs(0) - 1)
    def _():
        chunk = 16

        @pl.loop(0, waves // chunk)
        def _(i):
            piece = held[pl.ds(pl.multiple_of(i * chunk * slots, 8), chunk * slots), :]
            out_ref[pl.ds(i * chunk, chunk)] = piece.reshape(chunk, slots, 2 * width).astype(BF16)


def dft(grid, wave_order):
    fields, slots, _, lon_count = grid.shape
    waves = wave_order.shape[0]
    scale = 2.0 * math.pi / lon_count

    def angles(longitude):
        phase = wave_order[:, None] * longitude[None, :] % lon_count
        return phase.astype(F32) * scale

    part_a = angles(jnp.arange(lon_count // LANES, dtype=jnp.int32) * LANES)
    part_b = angles(jnp.arange(LANES, dtype=jnp.int32))
    norm = 1.0 / math.sqrt(lon_count)
    block = 4 if slots % 4 == 0 else (2 if slots % 2 == 0 else 1)
    whole = lambda x: pl.BlockSpec(x.shape, lambda i: (0, 0))
    tables = [jnp.cos(part_a) * norm, jnp.sin(part_a) * norm, jnp.cos(part_b), jnp.sin(part_b)]
    return pl.pallas_call(
        functools.partial(dft_kernel, slots, block),
        grid=(slots // block,),
        in_specs=[pl.BlockSpec((fields, block, 2, lon_count), lambda i: (0, i, 0, 0))]
        + [whole(x) for x in tables],
        out_specs=pl.BlockSpec((waves, slots, 4 * fields), lambda i: (0, 0, 0)),
        out_shape=jax.ShapeDtypeStruct((waves, slots, 4 * fields), BF16),
        scratch_shapes=[
            pltpu.VMEM((2 * waves, lon_count), BF16),
            pltpu.VMEM((waves * slots, 4 * fields), F32),
        ],
        compiler_params=pltpu.CompilerParams(vmem_limit_bytes=56 * 2**20),
    )(grid, *tables)


def spectral_kernel(
    rows_total, wave_ref, start_ref, block_ref, data_ref, legendre_ref, to_phys, to_slot, keep_code,
    mix_in, mix_out, implicit_ref, out_ref,
):
    i = pl.program_id(0)
    m = wave_ref[i]
    first = start_ref[i]
    owners, levels, _, slots, part = data_ref.shape
    lats = owners * slots
    width = levels * part
    mapped = [data_ref[:, v, 0].reshape(lats, part) for v in range(levels)]
    x = jnp.concatenate(mapped, 1)
    x = jnp.dot(to_phys[...], x, preferred_element_type=F32)
    lane = lax.broadcasted_iota(jnp.int32, (lats, width), 1)
    lat = lax.broadcasted_iota(jnp.int32, (lats, width), 0)
    north = lane % 2 == 0
    lat_ok = lat >= first
    sym = jnp.where(
        north, x + pltpu.roll(x, width - 1, 1), pltpu.roll(x, 1, 1) - x
    )
    sym = jnp.where(lat_ok, sym, 0.0).astype(BF16)
    basis = legendre_ref[0]
    y = jnp.dot(basis, sym, preferred_element_type=F32)
    y = jnp.where(keep_code[...] < rows_total - m, y, 0.0).astype(BF16)
    modal = jnp.dot(y, mix_in[...], preferred_element_type=F32)
    degree = (m + lax.broadcasted_iota(jnp.int32, (rows_total, 1), 0)).astype(F32)
    factor = degree * (degree + 1.0) / float(rows_total * (rows_total - 1))
    scaled = (modal / (1.0 + factor * implicit_ref[...])).astype(BF16)
    solved = jnp.dot(scaled, mix_out[...], preferred_element_type=F32).astype(BF16)
    o = lax.dot_general(basis, solved, (((0,), (0,)), ((), ())), preferred_element_type=F32)
    o = jnp.where(lat_ok, o, 0.0).astype(BF16)
    o = jnp.dot(to_slot[...], o, preferred_element_type=F32).astype(BF16)
    for v in range(levels):
        out_ref[:, v, 0] = o[:, v * part : (v + 1) * part].reshape(owners, slots, part)


def spectral(
    data, legendre, first_block, my_waves, my_starts, lat_order, modes_in, modes_out, implicit
):
    owners, levels, mine, slots, part = data.shape
    rows_total, lats = legendre.shape[1], legendre.shape[2]
    fields = part // 4
    width = levels * part
    order = jnp.arange(lats, dtype=jnp.int32)
    to_slot = (lat_order[:, None] == order[None, :]).astype(BF16)
    to_phys = to_slot.T
    lane = jnp.arange(width, dtype=jnp.int32)
    row = jnp.arange(rows_total, dtype=jnp.int32)
    keep_code = jnp.where(row[:, None] % 2 == lane[None, :] % 2, row[:, None], 2 * rows_total)
    modes = modes_in.shape[0]
    in_by_lane = modes_in.T.reshape(levels, fields, modes)
    sign = jnp.array([[1.0, 1.0], [1.0, -1.0]], F32)
    eye = jnp.eye(2, dtype=F32)
    mix_in = jnp.einsum("vfk,cd,hg->vcfhgdk", in_by_lane.astype(F32), eye, sign)
    mix_in = mix_in.reshape(width, 4 * modes).astype(BF16)
    out_by_lane = modes_out.reshape(levels, fields, modes)
    mix_out = jnp.einsum("vfk,cd,hg->gdkvcfh", out_by_lane.astype(F32), eye, eye)
    mix_out = mix_out.reshape(4 * modes, width).astype(BF16)
    implicit_lane = jnp.tile(implicit, 4)[None, :]
    block = pl.BlockSpec((owners, levels, 1, slots, part), lambda i, *_: (0, 0, i, 0, 0))
    whole = lambda x: pl.BlockSpec(x.shape, lambda i, *_: (0, 0))
    consts = [to_phys, to_slot, keep_code, mix_in, mix_out, implicit_lane]
    return pl.pallas_call(
        functools.partial(spectral_kernel, rows_total),
        grid_spec=pltpu.PrefetchScalarGridSpec(
            num_scalar_prefetch=3,
            grid=(mine,),
            in_specs=[
                block,
                pl.BlockSpec((1, rows_total, lats), lambda i, w, s, o: (o[0] + i, 0, 0)),
            ]
            + [whole(x) for x in consts],
            out_specs=block,
        ),
        out_shape=jax.ShapeDtypeStruct(data.shape, BF16),
        compiler_params=pltpu.CompilerParams(vmem_limit_bytes=56 * 2**20),
    )(my_waves, my_starts, first_block, data, legendre, *consts)


def spread_kernel(slots, block, data_ref, spread_ref, out_ref, held):
    step = pl.program_id(0)
    waves = data_ref.shape[0]
    width = data_ref.shape[2] // 2
    span = LANES

    @pl.when(step == 0)
    def _():
        chunk = 16

        @pl.loop(0, waves // chunk)
        def _(i):
            piece = data_ref[pl.ds(i * chunk, chunk)].astype(F32)
            held[pl.ds(pl.multiple_of(i * chunk * slots, 8), chunk * slots), :] = piece.reshape(
                chunk * slots, 2 * width
            )

    turned = [
        held[pl.ds(step * block + s, waves, stride=slots), :].T.astype(BF16) for s in range(block)
    ]
    for b in range(waves // span):
        part = slice(b * span, (b + 1) * span)
        lhs = jnp.concatenate(
            [jnp.concatenate([t[:width, part], t[width:, part]], 1) for t in turned], 0
        )
        got = jnp.dot(lhs, spread_ref[...], preferred_element_type=F32).astype(BF16)
        for s in range(block):
            out_ref[:, s, :, 2 * b * span : 2 * (b + 1) * span] = got[
                s * width : (s + 1) * width
            ].reshape(width // 2, 2, 2 * span)


def spread(data, fields):
    waves, slots, part = data.shape
    block = 4 if slots % 4 == 0 else (2 if slots % 2 == 0 else 1)
    span = LANES
    source = jnp.arange(2 * span, dtype=jnp.int32)
    goal = 2 * (source % span) + source // span
    matrix = (goal[:, None] == source[None, :]).astype(BF16)
    return pl.pallas_call(
        functools.partial(spread_kernel, slots, block),
        grid=(slots // block,),
        in_specs=[
            pl.BlockSpec(data.shape, lambda i: (0, 0, 0)),
            pl.BlockSpec(matrix.shape, lambda i: (0, 0)),
        ],
        out_specs=pl.BlockSpec((fields, block, 2, 2 * waves), lambda i: (0, i, 0, 0)),
        out_shape=jax.ShapeDtypeStruct((fields, slots, 2, 2 * waves), BF16),
        scratch_shapes=[pltpu.VMEM((waves * slots, part), F32)],
        compiler_params=pltpu.CompilerParams(vmem_limit_bytes=56 * 2**20),
    )(data, matrix)


def local(grid, lat_order, wave_order, trim, legendre, modes_in, modes_out, implicit):
    fields, slots = grid.shape[0], grid.shape[1]
    owners, levels = lax.axis_size("wave"), lax.axis_size("lev")
    mine = legendre.shape[0] // levels
    lev = lax.axis_index("lev")
    first = (lax.axis_index("wave") * levels + lev) * mine
    my_waves = lax.dynamic_slice_in_dim(wave_order, first, mine)
    my_starts = LBLK * jnp.sum(
        jnp.where(my_waves[:, None] == jnp.arange(trim.shape[0])[None, :], trim[None, :], 0), 1
    )
    spectra = dft(grid, wave_order)
    sent = lax.all_to_all(spectra, ("wave", "lev"), split_axis=0, concat_axis=0, tiled=True)
    data = sent.reshape(owners, levels, mine, slots, 4 * fields)
    back = spectral(
        data, legendre, (lev * mine)[None], my_waves, my_starts, lat_order, modes_in, modes_out, implicit
    )
    back = back.reshape(spectra.shape)
    back = lax.all_to_all(back, ("wave", "lev"), split_axis=0, concat_axis=0, tiled=True)
    return spread(back, fields)


def solution(mesh):
    in_specs = (
        P(("member", "lev"), "wave", None, None),
        P(),
        P(),
        P(),
        P("wave", None, None),
        P(),
        P(),
        P(),
    )
    out_specs = P(("member", "lev"), "wave", None, None)
    return jax.shard_map(local, mesh=mesh, in_specs=in_specs, out_specs=out_specs, check_vma=False)
```

```python
import functools
import math

import jax
import jax.numpy as jnp
from jax import lax
from jax.experimental import pallas as pl
from jax.experimental.pallas import tpu as pltpu
from jax.sharding import PartitionSpec as P

LBLK = 64
LANES = 128
CHUNKS = 2
F32 = jnp.float32
BF16 = jnp.bfloat16


def dft_kernel(slots, block, grid_ref, cos_a, sin_a, cos_b, sin_b, out_ref, table, held):
    step = pl.program_id(0)
    waves = cos_b.shape[0]
    fields = grid_ref.shape[0]
    width = 2 * fields

    @pl.when(step == 0)
    def _():
        for a in range(cos_a.shape[1]):
            ca, sa = cos_a[:, a : a + 1], sin_a[:, a : a + 1]
            cols = slice(a * LANES, (a + 1) * LANES)
            table[:waves, cols] = (ca * cos_b[...] - sa * sin_b[...]).astype(BF16)
            table[waves:, cols] = (-(sa * cos_b[...] + ca * sin_b[...])).astype(BF16)

    rows = jnp.concatenate(
        [grid_ref[:, s].reshape(width, grid_ref.shape[3]) for s in range(block)], 0
    )
    real = lax.dot_general(
        table[:waves], rows, (((1,), (1,)), ((), ())), preferred_element_type=F32
    )
    imag = lax.dot_general(
        table[waves:], rows, (((1,), (1,)), ((), ())), preferred_element_type=F32
    )
    for s in range(block):
        part = slice(s * width, (s + 1) * width)
        both = jnp.concatenate([real[:, part], imag[:, part]], 1)
        held[pl.ds(step * block + s, waves, stride=slots), :] = both

    @pl.when(step == pl.num_programs(0) - 1)
    def _():
        chunk = 16

        @pl.loop(0, waves // chunk)
        def _(i):
            piece = held[pl.ds(pl.multiple_of(i * chunk * slots, 8), chunk * slots), :]
            out_ref[pl.ds(i * chunk, chunk)] = piece.reshape(chunk, slots, 2 * width).astype(BF16)


def dft(grid, wave_order):
    fields, slots, _, lon_count = grid.shape
    waves = wave_order.shape[0]
    scale = 2.0 * math.pi / lon_count

    def angles(longitude):
        phase = wave_order[:, None] * longitude[None, :] % lon_count
        return phase.astype(F32) * scale

    part_a = angles(jnp.arange(lon_count // LANES, dtype=jnp.int32) * LANES)
    part_b = angles(jnp.arange(LANES, dtype=jnp.int32))
    norm = 1.0 / math.sqrt(lon_count)
    block = 4 if slots % 4 == 0 else (2 if slots % 2 == 0 else 1)
    whole = lambda x: pl.BlockSpec(x.shape, lambda i: (0, 0))
    tables = [jnp.cos(part_a) * norm, jnp.sin(part_a) * norm, jnp.cos(part_b), jnp.sin(part_b)]
    return pl.pallas_call(
        functools.partial(dft_kernel, slots, block),
        grid=(slots // block,),
        in_specs=[pl.BlockSpec((fields, block, 2, lon_count), lambda i: (0, i, 0, 0))]
        + [whole(x) for x in tables],
        out_specs=pl.BlockSpec((waves, slots, 4 * fields), lambda i: (0, 0, 0)),
        out_shape=jax.ShapeDtypeStruct((waves, slots, 4 * fields), BF16),
        scratch_shapes=[
            pltpu.VMEM((2 * waves, lon_count), BF16),
            pltpu.VMEM((waves * slots, 4 * fields), F32),
        ],
        compiler_params=pltpu.CompilerParams(vmem_limit_bytes=56 * 2**20),
        cost_estimate=pl.CostEstimate(
            flops=4 * waves * lon_count * fields * slots * 2,
            bytes_accessed=4 * grid.size,
            transcendentals=0,
        ),
    )(grid, *tables)


def spectral_kernel(
    rows_total, wave_ref, start_ref, block_ref, data_ref, legendre_ref, to_phys, to_slot, keep_code,
    mix_in, mix_out, implicit_ref, out_ref,
):
    i = pl.program_id(0)
    m = wave_ref[i]
    first = start_ref[i]
    owners, levels, _, slots, part = data_ref.shape
    lats = owners * slots
    width = levels * part
    mapped = [data_ref[:, v, 0].reshape(lats, part) for v in range(levels)]
    x = jnp.concatenate(mapped, 1)
    x = jnp.dot(to_phys[...], x, preferred_element_type=F32)
    lane = lax.broadcasted_iota(jnp.int32, (lats, width), 1)
    lat = lax.broadcasted_iota(jnp.int32, (lats, width), 0)
    north = lane % 2 == 0
    lat_ok = lat >= first
    sym = jnp.where(
        north, x + pltpu.roll(x, width - 1, 1), pltpu.roll(x, 1, 1) - x
    )
    sym = jnp.where(lat_ok, sym, 0.0).astype(BF16)
    basis = legendre_ref[0]
    y = lax.dot_general(basis, sym, (((0,), (0,)), ((), ())), preferred_element_type=F32)
    y = jnp.where(keep_code[...] < rows_total - m, y, 0.0).astype(BF16)
    modal = jnp.dot(y, mix_in[...], preferred_element_type=F32)
    degree = (m + lax.broadcasted_iota(jnp.int32, (rows_total, 1), 0)).astype(F32)
    factor = degree * (degree + 1.0) / float(rows_total * (rows_total - 1))
    scaled = (modal / (1.0 + factor * implicit_ref[...])).astype(BF16)
    solved = jnp.dot(scaled, mix_out[...], preferred_element_type=F32).astype(BF16)
    o = jnp.dot(basis, solved, preferred_element_type=F32)
    o = jnp.where(lat_ok, o, 0.0).astype(BF16)
    o = jnp.dot(to_slot[...], o, preferred_element_type=F32).astype(BF16)
    for v in range(levels):
        out_ref[:, v, 0] = o[:, v * part : (v + 1) * part].reshape(owners, slots, part)


def spectral(
    data, legendre, first_block, my_waves, my_starts, lat_order, modes_in, modes_out, implicit
):
    owners, levels, mine, slots, part = data.shape
    lats, rows_total = legendre.shape[1], legendre.shape[2]
    fields = part // 4
    width = levels * part
    order = jnp.arange(lats, dtype=jnp.int32)
    to_slot = (lat_order[:, None] == order[None, :]).astype(BF16)
    to_phys = to_slot.T
    lane = jnp.arange(width, dtype=jnp.int32)
    row = jnp.arange(rows_total, dtype=jnp.int32)
    keep_code = jnp.where(row[:, None] % 2 == lane[None, :] % 2, row[:, None], 2 * rows_total)
    modes = modes_in.shape[0]
    in_by_lane = modes_in.T.reshape(levels, fields, modes)
    sign = jnp.array([[1.0, 1.0], [1.0, -1.0]], F32)
    eye = jnp.eye(2, dtype=F32)
    mix_in = jnp.einsum("vfk,cd,hg->vcfhgdk", in_by_lane.astype(F32), eye, sign)
    mix_in = mix_in.reshape(width, 4 * modes).astype(BF16)
    out_by_lane = modes_out.reshape(levels, fields, modes)
    mix_out = jnp.einsum("vfk,cd,hg->gdkvcfh", out_by_lane.astype(F32), eye, eye)
    mix_out = mix_out.reshape(4 * modes, width).astype(BF16)
    implicit_lane = jnp.tile(implicit, 4)[None, :]
    block = pl.BlockSpec((owners, levels, 1, slots, part), lambda i, *_: (0, 0, i, 0, 0))
    whole = lambda x: pl.BlockSpec(x.shape, lambda i, *_: (0, 0))
    consts = [to_phys, to_slot, keep_code, mix_in, mix_out, implicit_lane]
    return pl.pallas_call(
        functools.partial(spectral_kernel, rows_total),
        grid_spec=pltpu.PrefetchScalarGridSpec(
            num_scalar_prefetch=3,
            grid=(mine,),
            in_specs=[
                block,
                pl.BlockSpec((1, lats, rows_total), lambda i, w, s, o: (o[0] + i, 0, 0)),
            ]
            + [whole(x) for x in consts],
            out_specs=block,
        ),
        out_shape=jax.ShapeDtypeStruct(data.shape, BF16),
        compiler_params=pltpu.CompilerParams(vmem_limit_bytes=56 * 2**20),
        cost_estimate=pl.CostEstimate(
            flops=4 * mine * width * (lats + rows_total) * (lats + width),
            bytes_accessed=2 * mine * rows_total * lats + 4 * data.size,
            transcendentals=0,
        ),
    )(my_waves, my_starts, first_block, data, legendre, *consts)


def spread_kernel(slots, block, parts, mine, *refs):
    data_refs, (spread_ref, out_ref, held) = refs[:parts], refs[parts:]
    step = pl.program_id(0)
    waves = held.shape[0] // slots
    width = held.shape[1] // 2
    span = LANES
    share = mine // parts

    @pl.when(step == 0)
    def _():
        for c in range(parts):

            @pl.loop(0, waves // mine)
            def _(d):
                piece = data_refs[c][pl.ds(d * share, share)].astype(F32)
                start = (d * mine + c * share) * slots
                if share * slots % 8 == 0:
                    start = pl.multiple_of(start, 8)
                held[pl.ds(start, share * slots), :] = piece.reshape(share * slots, 2 * width)

    turned = [
        held[pl.ds(step * block + s, waves, stride=slots), :].T.astype(BF16) for s in range(block)
    ]
    for b in range(waves // span):
        part = slice(b * span, (b + 1) * span)
        lhs = jnp.concatenate(
            [jnp.concatenate([t[:width, part], t[width:, part]], 1) for t in turned], 0
        )
        got = jnp.dot(lhs, spread_ref[...], preferred_element_type=F32).astype(BF16)
        for s in range(block):
            out_ref[:, s, :, 2 * b * span : 2 * (b + 1) * span] = got[
                s * width : (s + 1) * width
            ].reshape(width // 2, 2, 2 * span)


def spread(datas, fields, mine):
    slots, part = datas[0].shape[1:]
    waves = sum(d.shape[0] for d in datas)
    block = 4 if slots % 4 == 0 else (2 if slots % 2 == 0 else 1)
    span = LANES
    source = jnp.arange(2 * span, dtype=jnp.int32)
    goal = 2 * (source % span) + source // span
    matrix = (goal[:, None] == source[None, :]).astype(BF16)
    return pl.pallas_call(
        functools.partial(spread_kernel, slots, block, len(datas), mine),
        grid=(slots // block,),
        in_specs=[pl.BlockSpec(d.shape, lambda i: (0, 0, 0)) for d in datas]
        + [pl.BlockSpec(matrix.shape, lambda i: (0, 0))],
        out_specs=pl.BlockSpec((fields, block, 2, 2 * waves), lambda i: (0, i, 0, 0)),
        out_shape=jax.ShapeDtypeStruct((fields, slots, 2, 2 * waves), BF16),
        scratch_shapes=[pltpu.VMEM((waves * slots, part), F32)],
        compiler_params=pltpu.CompilerParams(vmem_limit_bytes=56 * 2**20),
    )(*datas, matrix)


def exchange(x):
    return lax.all_to_all(x, ("wave", "lev"), split_axis=0, concat_axis=0, tiled=True)


def local(grid, lat_order, wave_order, trim, legendre, modes_in, modes_out, implicit):
    fields, slots = grid.shape[0], grid.shape[1]
    owners, levels = lax.axis_size("wave"), lax.axis_size("lev")
    mine = legendre.shape[0] // levels
    lev = lax.axis_index("lev")
    first = (lax.axis_index("wave") * levels + lev) * mine
    my_waves = lax.dynamic_slice_in_dim(wave_order, first, mine)
    my_starts = LBLK * jnp.sum(
        jnp.where(my_waves[:, None] == jnp.arange(trim.shape[0])[None, :], trim[None, :], 0), 1
    )
    chunks = CHUNKS if mine % CHUNKS == 0 else 1
    share = mine // chunks
    orders = wave_order.reshape(owners * levels, chunks, share)
    turned = legendre.transpose(0, 2, 1)
    received = []
    for c in range(chunks):
        spectra = dft(grid, orders[:, c].reshape(-1))
        received.append(exchange(spectra))
    returned = []
    for c in range(chunks):
        data = received[c].reshape(owners, levels, share, slots, 4 * fields)
        mid = slice(c * share, (c + 1) * share)
        back = spectral(
            data, turned, (lev * mine + c * share)[None], my_waves[mid], my_starts[mid],
            lat_order, modes_in, modes_out, implicit,
        )
        returned.append(exchange(back.reshape(received[c].shape)))
    return spread(returned, fields, mine)


def solution(mesh):
    in_specs = (
        P(("member", "lev"), "wave", None, None),
        P(),
        P(),
        P(),
        P("wave", None, None),
        P(),
        P(),
        P(),
    )
    out_specs = P(("member", "lev"), "wave", None, None)
    return jax.shard_map(local, mesh=mesh, in_specs=in_specs, out_specs=out_specs, check_vma=False)
```
